32 devices in a mesh: cells: 8 (over z, y), dirs: 4 (over x, core).
Axes of the slice: x: 2, y: 2, z: 4, core: 2. Of those that a mesh axis runs over, the one named last changes fastest.
Arguments:
- incident: float32 [512, 6144], P('cells', 'dirs'), may hold values from -24 to 24
- scattering: float32 [512, 192], P('cells'), may hold values from 0.1 to 1
- translations: bfloat16 [8, 192, 192], replicated, may hold values from -1.5 to 1.5
- pair_sphere: int32 [512, 16], P('cells'), may hold values from 0 to 511, as said below
- pair_class: int32 [512, 16], P('cells'), may hold values from 0 to 7
- pair_weight: bfloat16 [512, 16], P('cells'), may hold values from 0.19921875 to 0.796875
- pair_mask: int32 [512, 16], P('cells'), may hold values from 0 to 1, as said below
Outputs:
- solution: float32 [512, 6144], P('cells', 'dirs')
- residual: float32 [512, 6144], P('cells', 'dirs')
- dual_residual: float32 [512, 6144], P('cells', 'dirs')
- direction: float32 [512, 6144], P('cells', 'dirs')
The draws below stay inside these ranges and needn't reach their ends.
Inputs may be any that keep to these rules, and one draw needn't show every extreme that they name: `pair_sphere`: sphere ids are cell-major: cell c holds spheres 64 c to 64 (c + 1) - 1, and the cells form a cycle. The slots of one sphere name distinct spheres, never the sphere itself; each named sphere lies in the sphere's own cell, or among the last 32 spheres of the previous cell, or among the first 32 spheres of the next cell. In every cell the first sphere names sphere 64 - 32 of the previous cell and the last sphere names sphere 32 - 1 of the next, both in live slots. `pair_mask`: the live slots of a sphere come first; the first and the last sphere of every cell have all 16 slots live, every sphere at least 8.
All inputs are finite; a program needn't handle non-finite values.
Results may differ from the reference program's by a relative error of at most 0.0003.
The reference program's roundings to bfloat16 on the way count: a program that leaves them out, or rounds other values in their place, can miss the bound.
Values may be sent and summed in bfloat16 or wider, within the bound.
A program may use at most 64 MiB of HBM per device.

```python
import math
import jax
import jax.numpy as jnp
from jax import lax

C = 192
DIRS = 32
S_DEV = 64
BAND = 32
NB = 16
CLASSES = 8
SPHERES = 512


def draw_incident(key, part):
    rows = jnp.arange(SPHERES, dtype=jnp.int32)
    cell_count = SPHERES // S_DEV
    place = (rows // S_DEV).astype(jnp.float32) / jnp.float32(max(cell_count - 1, 1))
    shape = (SPHERES, DIRS * C)
    common_key = jax.random.fold_in(key, 11)
    own_key = jax.random.fold_in(key, 12)
    common = jnp.clip(jax.random.normal(common_key, (1, DIRS * C), jnp.float32), -4.2, 4.2)
    own = jnp.clip(jax.random.normal(own_key, shape, jnp.float32), -4.2, 4.2)
    scale = jnp.float32(4.0) ** place
    values = jnp.float32(0.6) * common + jnp.float32(0.8) * own
    return (values * scale[:, None]).astype(jnp.float32)


def draw_scattering(key, part):
    rows = jnp.arange(SPHERES, dtype=jnp.int32)
    cell_count = SPHERES // S_DEV
    place = (rows // S_DEV).astype(jnp.float32) / jnp.float32(max(cell_count - 1, 1))
    spread = jax.random.uniform(jax.random.fold_in(key, 21), (SPHERES, C), jnp.float32, 0.0, 1.0)
    exponent = jnp.float32(0.7) * place[:, None] + jnp.float32(0.3) * spread
    return (jnp.float32(10.0) ** (-exponent)).astype(jnp.float32)


def draw_translations(key, part):
    noise = jnp.clip(jax.random.normal(jax.random.fold_in(key, 31), (CLASSES, C, C), jnp.float32), -6.0, 6.0)
    noise = noise * jnp.float32(C) ** (-0.5)
    diagonal = jax.random.uniform(jax.random.fold_in(key, 32), (CLASSES, 1, C), jnp.float32, 0.1, 0.3)
    index = jnp.arange(C, dtype=jnp.int32)
    eye = (index[:, None] == index[None, :]).astype(jnp.float32)
    return (noise + eye[None, :, :] * diagonal).astype(jnp.bfloat16)


def draw_pair_sphere(key, part):
    rows = jnp.arange(SPHERES, dtype=jnp.int32)
    within = rows % S_DEV
    owner = rows // S_DEV
    cell_count = SPHERES // S_DEV
    extent = S_DEV + 2 * BAND
    upper_pick = extent // NB - 1
    slots = jnp.arange(NB, dtype=jnp.int32)
    picks = jax.random.randint(key, (SPHERES, NB), 0, upper_pick, dtype=jnp.int32)
    prev_slot = (S_DEV + BAND - 1) % NB
    prev_pick = (S_DEV + BAND - 1) // NB
    next_slot = (BAND - 1) % NB
    next_pick = (BAND - 1) // NB
    picks = jnp.where((within == 0)[:, None] & (slots == prev_slot)[None, :], prev_pick, picks)
    picks = jnp.where((within == S_DEV - 1)[:, None] & (slots == next_slot)[None, :], next_pick, picks)
    spot = (BAND + within[:, None] + 1 + slots[None, :] + NB * picks) % extent
    target_cell = jnp.where(spot < BAND, owner[:, None] - 1, jnp.where(spot < BAND + S_DEV, owner[:, None], owner[:, None] + 1))
    target_cell = target_cell % cell_count
    target_local = jnp.where(spot < BAND, S_DEV - BAND + spot, jnp.where(spot < BAND + S_DEV, spot - BAND, spot - BAND - S_DEV))
    return (target_cell * S_DEV + target_local).astype(jnp.int32)


def draw_pair_mask(key, part):
    rows = jnp.arange(SPHERES, dtype=jnp.int32)
    within = rows % S_DEV
    live = jax.random.randint(key, (SPHERES,), NB // 2, NB + 1, dtype=jnp.int32)
    live = jnp.where((within == 0) | (within == S_DEV - 1), NB, live)
    slots = jnp.arange(NB, dtype=jnp.int32)
    return (slots[None, :] < live[:, None]).astype(jnp.int32)


def set_ends(values, key, least, largest):
    spot = [jax.random.randint(jax.random.fold_in(key, axis), (), 0, length) for axis, length in enumerate(values.shape)]
    widest = values.shape.index(max(values.shape))
    beside = spot[:widest] + [(spot[widest] + 1) % values.shape[widest]] + spot[widest + 1:]
    return values.at[tuple(spot)].set(least).at[tuple(beside)].set(largest)


def block_levels(stream_key, shape, cuts, least, high):
    level = 1.0
    for axis_at, blocks in cuts:
        steps = jax.random.uniform(jax.random.fold_in(jax.random.fold_in(stream_key, 6), axis_at), (blocks,), jnp.float32, least / len(cuts), high / len(cuts))
        level = level * jnp.repeat(jnp.exp(steps), shape[axis_at] // blocks).reshape((-1,) + (1,) * (len(shape) - 1 - axis_at))
    return level


def setup_inputs(seed: int = 0) -> dict:
    key_list = jax.random.split(jax.random.key(seed), 8)
    return {
        "incident": draw_incident(jax.random.fold_in(key_list[7], 71), 0),
        "scattering": draw_scattering(jax.random.fold_in(key_list[7], 71), 0),
        "translations": draw_translations(jax.random.fold_in(key_list[7], 71), 0),
        "pair_sphere": draw_pair_sphere(jax.random.fold_in(key_list[7], 71), 0),
        "pair_class": set_ends(jax.random.randint(key_list[4], (SPHERES, NB), 0, CLASSES), jax.random.fold_in(key_list[4], 1), 0, CLASSES - 1).astype(jnp.int32),
        "pair_weight": jnp.clip(jnp.exp(math.log(0.796875) - 1.3862944 * jax.random.uniform(key_list[5], (SPHERES, NB), jnp.float32) ** block_levels(key_list[5], (SPHERES, NB), ((0, 8),), -0.2, 0.2)), 0.19921875, 0.796875).astype(jnp.bfloat16),
        "pair_mask": draw_pair_mask(jax.random.fold_in(key_list[7], 71), 0),
    }


def reference(incident, scattering, translations, pair_sphere, pair_class, pair_weight, pair_mask):
    cell_count = SPHERES // S_DEV
    columns = incident.shape[1]
    groups = columns // C
    strength = pair_weight.astype(jnp.float32) * pair_mask.astype(jnp.float32)
    source = incident.astype(jnp.bfloat16)
    gain = jnp.tile(scattering, (1, groups))
    sphere_cells = pair_sphere.reshape(cell_count, S_DEV, NB)
    class_cells = pair_class.reshape(cell_count, S_DEV, NB)
    weight_cells = strength.reshape(cell_count, S_DEV, NB)

    def cell_primal(pieces):
        targets, kinds, weights = pieces
        gathered = source[targets].astype(jnp.float32)
        total = jnp.zeros((S_DEV, columns), jnp.float32)
        for klass in range(CLASSES):
            factor = jnp.where(kinds == klass, weights, jnp.float32(0.0))
            summed = jnp.einsum("sm,smd->sd", factor, gathered, precision=lax.Precision.HIGHEST).astype(jnp.bfloat16)
            moved = jnp.dot(summed.reshape(S_DEV * groups, C), translations[klass], preferred_element_type=jnp.float32)
            total = total + moved.reshape(S_DEV, columns)
        return total

    coupled = lax.map(cell_primal, (sphere_cells, class_cells, weight_cells)).reshape(SPHERES, columns)
    image = incident - gain * coupled
    weighted = (gain * incident).astype(jnp.bfloat16)
    weighted_cells = weighted.reshape(cell_count, S_DEV, columns)

    def cell_dual(back, pieces):
        local_rows, targets, kinds, weights = pieces
        moved_all = []
        for klass in range(CLASSES):
            moved = jnp.dot(local_rows.reshape(S_DEV * groups, C), translations[klass].T, preferred_element_type=jnp.float32)
            moved_all.append(moved.reshape(S_DEV, columns))
        stacked = jnp.stack(moved_all, axis=0)
        picks = jnp.where(kinds[:, :, None] == jnp.arange(CLASSES, dtype=jnp.int32)[None, None, :], weights[:, :, None], jnp.float32(0.0))
        contrib = jnp.einsum("smk,ksd->smd", picks, stacked, precision=lax.Precision.HIGHEST)
        back = back.at[targets.reshape(-1)].add(contrib.reshape(S_DEV * NB, columns))
        return back, None

    back, unused = lax.scan(cell_dual, jnp.zeros((SPHERES, columns), jnp.float32), (weighted_cells, sphere_cells, class_cells, weight_cells))
    dual_image = incident - back
    norm_old = jnp.sum(incident * incident)
    curvature = jnp.sum(incident * image)
    step_size = norm_old / curvature
    solution = step_size * incident
    residual = incident - step_size * image
    dual_residual = incident - step_size * dual_image
    norm_new = jnp.sum(residual * dual_residual)
    direction = residual + (norm_new / norm_old) * incident
    return (solution, residual, dual_residual, direction)
```

```python
import functools
import jax
import jax.numpy as jnp
from jax import lax
from jax.experimental import pallas as pl
from jax.experimental.pallas import tpu as pltpu
from jax.sharding import PartitionSpec as P

F32 = jnp.float32
BF16 = jnp.bfloat16
STRIDE = 256


def folded(x):
    rows, width = x.shape
    y = jnp.sum(x.reshape(rows // 8, 8, width), axis=0)
    out = y[:, :128]
    for at in range(128, width, 128):
        out = out + y[:, at : at + 128]
    return out


def kernel(
    cells,
    dirs,
    inc_ref,
    sc_ref,
    tr_ref,
    ps_ref,
    pc_ref,
    pw_ref,
    pm_ref,
    img_ref,
    dual_ref,
    coef_ref,
    send,
    from_prev,
    from_next,
    meta,
    meta_prev,
    meta_next,
    gain,
    pick,
    dpick,
    te,
    to,
    tet,
    tot,
    gs,
    ghi,
    glo,
    red_d,
    red_c,
    ssem,
    rsem,
    msem,
    mrsem,
    dssem,
    drsem,
    cssem,
    crsem,
):
    rows, columns = inc_ref.shape
    band = rows // 2
    classes, order, _ = tr_ref.shape
    slots = ps_ref.shape[1]
    wide = 2 * order
    pairs = columns // wide
    me = lax.axis_index("cells")
    my_dir = lax.axis_index("dirs")
    right = lax.rem(me + 1, cells)
    left = lax.rem(me + cells - 1, cells)

    barrier = pltpu.get_barrier_semaphore()

    def greet_cell(t, c):
        pl.semaphore_signal(
            barrier, inc=1, device_id=(lax.rem(me + t, cells), my_dir), device_id_type=pl.DeviceIdType.MESH
        )
        return c

    def greet_dir(t, c):
        pl.semaphore_signal(
            barrier, inc=1, device_id=(me, lax.rem(my_dir + t, dirs)), device_id_type=pl.DeviceIdType.MESH
        )
        return c

    lax.fori_loop(1, cells, greet_cell, 0)
    lax.fori_loop(1, dirs, greet_dir, 0)

    gain[:, 0:order] = sc_ref[...]
    gain[:, order:wide] = sc_ref[...]
    g = gain[...]
    for p in range(pairs):
        x = inc_ref[:, p * wide : (p + 1) * wide]
        src = x.astype(BF16)
        send[p, 0:band, :] = src[0:band]
        send[p, band : band + rows, :] = (g * x).astype(BF16)
        send[p, band + rows :, :] = src[band:]

    ps = ps_ref[...]
    owner = ps // rows
    within = ps - owner * rows
    off = owner - me
    is_own = off == 0
    is_next = (off == 1) | (off == 1 - cells)
    place = jnp.where(is_own, band + within, jnp.where(is_next, band + rows + within, within - band))
    code = (pc_ref[...] * STRIDE + place).astype(F32)
    strength = pw_ref[...].astype(F32) * pm_ref[...].astype(F32)
    meta[0:slots, :] = jnp.concatenate([code, code], axis=0).T
    meta[slots : 2 * slots, :] = jnp.concatenate([strength, strength], axis=0).T

    pl.semaphore_wait(barrier, cells - 1 + dirs - 1)

    def to_right(p):
        return pltpu.make_async_remote_copy(
            src_ref=send.at[p, band : 2 * band + rows, :],
            dst_ref=from_prev.at[p],
            send_sem=ssem.at[0, p],
            recv_sem=rsem.at[0, p],
            device_id=(right, my_dir),
            device_id_type=pl.DeviceIdType.MESH,
        )

    def to_left(p):
        return pltpu.make_async_remote_copy(
            src_ref=send.at[p, 0 : band + rows, :],
            dst_ref=from_next.at[p],
            send_sem=ssem.at[1, p],
            recv_sem=rsem.at[1, p],
            device_id=(left, my_dir),
            device_id_type=pl.DeviceIdType.MESH,
        )

    def meta_copy(i, dst, who):
        return pltpu.make_async_remote_copy(
            src_ref=meta,
            dst_ref=dst,
            send_sem=msem.at[i],
            recv_sem=mrsem.at[i],
            device_id=(who, my_dir),
            device_id_type=pl.DeviceIdType.MESH,
        )

    meta_right = meta_copy(0, meta_prev, right)
    meta_left = meta_copy(1, meta_next, left)
    meta_right.start()
    meta_left.start()
    for p in range(pairs):
        to_right(p).start()
        to_left(p).start()

    gap = STRIDE - order

    def place_class(k, c):
        te[k] = jnp.zeros((STRIDE, STRIDE), BF16)
        te[k, 0:order, 0:order] = tr_ref[k]
        full = te[k].astype(F32)
        to[k] = pltpu.roll(pltpu.roll(full, gap, 0), gap, 1).astype(BF16)
        turned = full.T
        tet[k] = turned.astype(BF16)
        tot[k] = pltpu.roll(pltpu.roll(turned, gap, 0), gap, 1).astype(BF16)
        return c

    lax.fori_loop(0, classes, place_class, 0)

    extent = rows + 2 * band
    step = 16
    lane = lax.broadcasted_iota(jnp.int32, (step, extent), 1).astype(F32)
    for b in range(rows // step):
        at = b * step
        cb = [jnp.broadcast_to(code[at : at + step, m : m + 1], (step, extent)) - lane for m in range(slots)]
        sb = [jnp.broadcast_to(strength[at : at + step, m : m + 1], (step, extent)) for m in range(slots)]
        for k in range(classes):
            acc = jnp.zeros((step, extent), F32)
            for m in range(slots):
                acc = acc + jnp.where(cb[m] == F32(k * STRIDE), sb[m], F32(0.0))
            pick[k * rows + at : k * rows + at + step, :] = acc.astype(BF16)

    meta_right.wait_recv()
    meta_left.wait_recv()
    low = lax.broadcasted_iota(jnp.int32, (slots, extent), 1) < rows
    code_a = jnp.where(low, meta_prev[0:slots, :] - F32(band + rows), meta[0:slots, :] - F32(band))
    str_a = jnp.where(low, meta_prev[slots : 2 * slots, :], meta[slots : 2 * slots, :])
    code_b = meta_next[0:slots, :] + F32(band)
    str_b = meta_next[slots : 2 * slots, :]
    for b in range(rows // step):
        at = b * step
        sub = lax.broadcasted_iota(jnp.int32, (step, extent), 0).astype(F32) + F32(at)
        for cc, ss, lo_lane, width in ((code_a, str_a, 0, extent), (code_b, str_b, extent, rows)):
            cb = [jnp.broadcast_to(cc[m : m + 1, :], (step, extent)) - sub for m in range(slots)]
            for k in range(classes):
                acc = jnp.zeros((step, extent), F32)
                for m in range(slots):
                    sm = jnp.broadcast_to(ss[m : m + 1, :], (step, extent))
                    acc = acc + jnp.where(cb[m] == F32(k * STRIDE), sm, F32(0.0))
                dpick[k * rows + at : k * rows + at + step, lo_lane : lo_lane + width] = acc[:, :width].astype(BF16)

    sums = [jnp.zeros((8, 128), F32) for _ in range(4)]
    for p in range(pairs):
        to_right(p).wait_recv()
        to_left(p).wait_recv()
        around = jnp.concatenate(
            [from_prev[p, rows:, :], send[p, 0:band, :], send[p, band + rows :, :], from_next[p, 0:band, :]], axis=0
        )
        gs[...] = jnp.dot(pick[...], around, preferred_element_type=F32).astype(BF16)
        spread = jnp.concatenate(
            [from_prev[p, 0:rows, :], send[p, band : band + rows, :], from_next[p, band:, :]], axis=0
        )
        whole = jnp.dot(dpick[...], spread, preferred_element_type=F32)
        hi = whole.astype(BF16)
        ghi[...] = hi
        glo[...] = (whole - hi.astype(F32)).astype(BF16)
        even = jnp.zeros((rows, STRIDE), F32)
        odd = jnp.zeros((rows, STRIDE), F32)
        deven = jnp.zeros((2 * rows, STRIDE), F32)
        dodd = jnp.zeros((2 * rows, STRIDE), F32)
        skip = wide - STRIDE
        for k in range(classes):
            r = slice(k * rows, (k + 1) * rows)
            even = even + jnp.dot(gs[r, 0:STRIDE], te[k], preferred_element_type=F32)
            odd = odd + jnp.dot(gs[r, skip:], to[k], preferred_element_type=F32)
            both = jnp.concatenate([ghi[r, :], glo[r, :]], axis=0)
            deven = deven + jnp.dot(both[:, 0:STRIDE], tet[k], preferred_element_type=F32)
            dodd = dodd + jnp.dot(both[:, skip:], tot[k], preferred_element_type=F32)
        de = deven[:rows] + deven[rows:]
        do = dodd[:rows] + dodd[rows:]
        mid = STRIDE - skip
        coupled = jnp.concatenate([even[:, :skip], even[:, skip:] + odd[:, :mid], odd[:, mid:]], axis=1)
        back = jnp.concatenate([de[:, :skip], de[:, skip:] + do[:, :mid], do[:, mid:]], axis=1)
        x = inc_ref[:, p * wide : (p + 1) * wide]
        image = x - gain[...] * coupled
        dual = x - back
        img_ref[:, p * wide : (p + 1) * wide] = image
        dual_ref[:, p * wide : (p + 1) * wide] = dual
        sums[0] = sums[0] + folded(x * x)
        sums[1] = sums[1] + folded(x * image)
        sums[2] = sums[2] + folded(x * dual)
        sums[3] = sums[3] + folded(image * dual)

    mine = jnp.concatenate(
        [jnp.sum(s, axis=0, keepdims=True) for s in sums] + [jnp.zeros((4, 128), F32)], axis=0
    )
    red_d[my_dir] = mine

    def dir_copy(t, slot):
        return pltpu.make_async_remote_copy(
            src_ref=red_d.at[slot],
            dst_ref=red_d.at[slot],
            send_sem=dssem.at[t],
            recv_sem=drsem.at[slot],
            device_id=(me, lax.rem(my_dir + t, dirs)),
            device_id_type=pl.DeviceIdType.MESH,
        )

    def cell_copy(t, slot):
        return pltpu.make_async_remote_copy(
            src_ref=red_c.at[slot],
            dst_ref=red_c.at[slot],
            send_sem=cssem.at[t],
            recv_sem=crsem.at[slot],
            device_id=(lax.rem(me + t, cells), my_dir),
            device_id_type=pl.DeviceIdType.MESH,
        )

    for t in range(1, dirs):
        dir_copy(t, my_dir).start()
    for t in range(1, dirs):
        dir_copy(t, lax.rem(my_dir + t, dirs)).wait_recv()
    red_c[me] = jnp.sum(red_d[...], axis=0)

    def cell_start(t, c):
        cell_copy(t, me).start()
        return c

    def cell_wait(t, c):
        cell_copy(t, lax.rem(me + t, cells)).wait_recv()
        return c

    lax.fori_loop(1, cells, cell_start, 0)
    lax.fori_loop(1, cells, cell_wait, 0)
    total = jnp.sum(jnp.sum(red_c[...], axis=0), axis=1, keepdims=True)
    norm_old = total[0:1]
    along_image = total[1:2]
    along_dual = total[2:3]
    cross = total[3:4]
    size = norm_old / along_image
    norm_new = norm_old - size * (along_image + along_dual) + size * size * cross
    ratio = norm_new / norm_old
    coef_ref[0:1, :] = jnp.broadcast_to(size, (1, 128))
    coef_ref[1:2, :] = jnp.broadcast_to(ratio, (1, 128))
    coef_ref[2:8, :] = jnp.zeros((6, 128), F32)

    meta_right.wait_send()
    meta_left.wait_send()
    for p in range(pairs):
        to_right(p).wait_send()
        to_left(p).wait_send()
    for t in range(1, dirs):
        dir_copy(t, my_dir).wait_send()

    def cell_sent(t, c):
        cell_copy(t, me).wait_send()
        return c

    lax.fori_loop(1, cells, cell_sent, 0)


def on_device(cells, dirs, incident, scattering, translations, pair_sphere, pair_class, pair_weight, pair_mask):
    rows, columns = incident.shape
    classes, order, _ = translations.shape
    slots = pair_sphere.shape[1]
    wide = 2 * order
    pairs = columns // wide
    vmem = pl.BlockSpec(memory_space=pltpu.VMEM)
    image, dual_image, coef = pl.pallas_call(
        functools.partial(kernel, cells, dirs),
        out_shape=(
            jax.ShapeDtypeStruct((rows, columns), F32),
            jax.ShapeDtypeStruct((rows, columns), F32),
            jax.ShapeDtypeStruct((8, 128), F32),
        ),
        in_specs=[vmem] * 7,
        out_specs=(vmem, vmem, vmem),
        scratch_shapes=[
            pltpu.VMEM((pairs, 2 * rows, wide), BF16),
            pltpu.VMEM((pairs, 3 * rows // 2, wide), BF16),
            pltpu.VMEM((pairs, 3 * rows // 2, wide), BF16),
            pltpu.VMEM((2 * slots, 2 * rows), F32),
            pltpu.VMEM((2 * slots, 2 * rows), F32),
            pltpu.VMEM((2 * slots, 2 * rows), F32),
            pltpu.VMEM((rows, wide), F32),
            pltpu.VMEM((classes * rows, 2 * rows), BF16),
            pltpu.VMEM((classes * rows, 3 * rows), BF16),
            pltpu.VMEM((classes, STRIDE, STRIDE), BF16),
            pltpu.VMEM((classes, STRIDE, STRIDE), BF16),
            pltpu.VMEM((classes, STRIDE, STRIDE), BF16),
            pltpu.VMEM((classes, STRIDE, STRIDE), BF16),
            pltpu.VMEM((classes * rows, wide), BF16),
            pltpu.VMEM((classes * rows, wide), BF16),
            pltpu.VMEM((classes * rows, wide), BF16),
            pltpu.VMEM((dirs, 8, 128), F32),
            pltpu.VMEM((cells, 8, 128), F32),
            pltpu.SemaphoreType.DMA((2, pairs)),
            pltpu.SemaphoreType.DMA((2, pairs)),
            pltpu.SemaphoreType.DMA((2,)),
            pltpu.SemaphoreType.DMA((2,)),
            pltpu.SemaphoreType.DMA((dirs,)),
            pltpu.SemaphoreType.DMA((dirs,)),
            pltpu.SemaphoreType.DMA((cells,)),
            pltpu.SemaphoreType.DMA((cells,)),
        ],
        compiler_params=pltpu.CompilerParams(
            collective_id=0, has_side_effects=True, vmem_limit_bytes=32 * 1024 * 1024
        ),
    )(incident, scattering, translations, pair_sphere, pair_class, pair_weight, pair_mask)
    size = coef[0, 0]
    ratio = coef[1, 0]
    residual = incident - size * image
    return (size * incident, residual, incident - size * dual_image, residual + ratio * incident)


def solution(mesh):
    cells, dirs = mesh.shape["cells"], mesh.shape["dirs"]
    split = P("cells", "dirs")
    by_cell = P("cells", None)
    return jax.shard_map(
        functools.partial(on_device, cells, dirs),
        mesh=mesh,
        in_specs=(split, by_cell, P(), by_cell, by_cell, by_cell, by_cell),
        out_specs=(split, split, split, split),
        check_vma=False,
    )
```

```python
import functools
import jax
import jax.numpy as jnp
from jax import lax
from jax.experimental import pallas as pl
from jax.experimental.pallas import tpu as pltpu
from jax.sharding import PartitionSpec as P

F32 = jnp.float32
BF16 = jnp.bfloat16
STRIDE = 256


def folded(x):
    rows, width = x.shape
    y = jnp.sum(x.reshape(rows // 8, 8, width), axis=0)
    out = y[:, :128]
    for at in range(128, width, 128):
        out = out + y[:, at : at + 128]
    return out


def kernel(
    cells,
    dirs,
    inc_hbm,
    sc_hbm,
    tr_hbm,
    ps_hbm,
    pc_hbm,
    pw_hbm,
    pm_hbm,
    img_hbm,
    dual_hbm,
    coef_ref,
    inc_ref,
    img_ref,
    dual_ref,
    sc_ref,
    tr_ref,
    ps_ref,
    pc_ref,
    pw_ref,
    pm_ref,
    send,
    near,
    far,
    meta,
    meta_near,
    meta_far,
    gain,
    pick,
    dpick,
    te,
    to,
    tet,
    tot,
    gs,
    ghi,
    glo,
    red,
    isem,
    osem,
    lsem,
    ssem,
    rsem,
    msem,
    mrsem,
    fssem,
    frsem,
    tssem,
    trsem,
):
    rows, columns = inc_ref.shape
    band = rows // 2
    classes, order, _ = tr_ref.shape
    slots = ps_ref.shape[0]
    wide = 2 * order
    pairs = columns // wide
    me = lax.axis_index("cells")
    my_dir = lax.axis_index("dirs")
    devices = cells * dirs
    here = me * dirs + my_dir
    odd_cell = lax.rem(me, 2)
    partner = me + 1 - 2 * odd_cell
    across = lax.rem(me - 1 + 2 * odd_cell + cells, cells)
    onward = lax.rem(me + 2 - 4 * odd_cell + cells, cells)

    def peer(t):
        other = lax.rem(here + t, devices)
        return (other // dirs, lax.rem(other, dirs)), other

    small = [
        pltpu.make_async_copy(a, b, lsem.at[i])
        for i, (a, b) in enumerate(
            (
                (sc_hbm, sc_ref),
                (ps_hbm, ps_ref),
                (pc_hbm, pc_ref),
                (pw_hbm, pw_ref),
                (pm_hbm, pm_ref),
                (tr_hbm, tr_ref),
            )
        )
    ]

    def incident_in(p):
        cut = (slice(None), slice(p * wide, (p + 1) * wide))
        return pltpu.make_async_copy(inc_hbm.at[cut], inc_ref.at[cut], isem.at[p])

    def results_out(p):
        cut = (slice(None), slice(p * wide, (p + 1) * wide))
        return (
            pltpu.make_async_copy(img_ref.at[cut], img_hbm.at[cut], osem.at[0, p]),
            pltpu.make_async_copy(dual_ref.at[cut], dual_hbm.at[cut], osem.at[1, p]),
        )

    barrier = pltpu.get_barrier_semaphore()

    def greet(t, c):
        pl.semaphore_signal(barrier, inc=1, device_id=peer(t)[0], device_id_type=pl.DeviceIdType.MESH)
        return c

    lax.fori_loop(1, devices, greet, 0)
    for copy in small[:5]:
        copy.start()
    for p in range(pairs):
        incident_in(p).start()
    small[5].start()

    for copy in small[1:5]:
        copy.wait()
    ps = ps_ref[...]
    owner = ps // rows
    within = ps - owner * rows
    is_own = owner == me
    is_near = owner == partner
    code = (
        pc_ref[...] * STRIDE + jnp.where(is_near, within, jnp.where(is_own, rows + within, 2 * rows + within))
    ).astype(F32)
    place = jnp.where(
        is_near,
        within - band * odd_cell,
        jnp.where(is_own, band + within, rows + band + within - band * (1 - odd_cell)),
    )
    column = (pc_ref[...] * STRIDE + place).astype(F32)
    strength = pw_ref[...].astype(F32) * pm_ref[...].astype(F32)
    meta[0:slots, :] = jnp.concatenate([code, code], axis=1)
    meta[slots : 2 * slots, :] = jnp.concatenate([strength, strength], axis=1)

    small[0].wait()
    gain[:, 0:order] = sc_ref[...]
    gain[:, order:wide] = sc_ref[...]
    g = gain[...]

    def fill(p):
        incident_in(p).wait()
        x = inc_ref[:, p * wide : (p + 1) * wide]
        src = x.astype(BF16)
        send[p, 0:band, :] = src[0:band]
        send[p, band : band + rows, :] = (g * x).astype(BF16)
        send[p, band + rows :, :] = src[band:]

    fill(0)
    pl.semaphore_wait(barrier, devices - 1)

    def to_partner(p):
        return pltpu.make_async_remote_copy(
            src_ref=send.at[p],
            dst_ref=near.at[p],
            send_sem=ssem.at[p],
            recv_sem=rsem.at[p],
            device_id=(partner, my_dir),
            device_id_type=pl.DeviceIdType.MESH,
        )

    pass_on = pl.multiple_of(band * (1 - odd_cell), band)

    def forward(p):
        return pltpu.make_async_remote_copy(
            src_ref=near.at[p, pl.ds(pass_on, band + rows), :],
            dst_ref=far.at[p],
            send_sem=fssem.at[p],
            recv_sem=frsem.at[p],
            device_id=(onward, my_dir),
            device_id_type=pl.DeviceIdType.MESH,
        )

    def meta_copy(i, dst, who):
        return pltpu.make_async_remote_copy(
            src_ref=meta,
            dst_ref=dst,
            send_sem=msem.at[i],
            recv_sem=mrsem.at[i],
            device_id=(who, my_dir),
            device_id_type=pl.DeviceIdType.MESH,
        )

    meta_a = meta_copy(0, meta_near, partner)
    meta_b = meta_copy(1, meta_far, across)
    meta_b.start()
    meta_a.start()
    for p in range(pairs):
        if p > 0:
            fill(p)
        to_partner(p).start()

    both = jnp.concatenate([column, strength], axis=0)
    both = jnp.concatenate([both, both], axis=1)
    flat = jnp.concatenate([both] * (128 // (2 * slots)), axis=0).T
    code = flat[0:rows, 0:slots]
    strength = flat[0:rows, slots : 2 * slots]
    small[5].wait()

    gap = STRIDE - order

    def place_class(k, c):
        te[k] = jnp.zeros((STRIDE, STRIDE), BF16)
        te[k, 0:order, 0:order] = tr_ref[k]
        full = te[k].astype(F32)
        to[k] = pltpu.roll(pltpu.roll(full, gap, 0), gap, 1).astype(BF16)
        turned = full.T
        tet[k] = turned.astype(BF16)
        tot[k] = pltpu.roll(pltpu.roll(turned, gap, 0), gap, 1).astype(BF16)
        return c

    lax.fori_loop(0, classes, place_class, 0)

    extent = rows + 2 * band
    step = 16
    lane = lax.broadcasted_iota(jnp.int32, (step, extent), 1).astype(F32)
    for b in range(rows // step):
        at = b * step
        cb = [jnp.broadcast_to(code[at : at + step, m : m + 1], (step, extent)) - lane for m in range(slots)]
        sb = [jnp.broadcast_to(strength[at : at + step, m : m + 1], (step, extent)) for m in range(slots)]
        for k in range(classes):
            acc = jnp.zeros((step, extent), F32)
            for m in range(slots):
                acc = acc + jnp.where(cb[m] == F32(k * STRIDE), sb[m], F32(0.0))
            pick[k * rows + at : k * rows + at + step, :] = acc.astype(BF16)

    meta_a.wait_recv()
    meta_b.wait_recv()
    low = lax.broadcasted_iota(jnp.int32, (slots, extent), 1) < rows
    code_a = jnp.where(low, meta_near[0:slots, :], meta[0:slots, :] - F32(rows))
    str_a = jnp.where(low, meta_near[slots : 2 * slots, :], meta[slots : 2 * slots, :])
    code_b = meta_far[0:slots, :] - F32(2 * rows)
    str_b = meta_far[slots : 2 * slots, :]
    for b in range(rows // step):
        at = b * step
        sub = lax.broadcasted_iota(jnp.int32, (step, extent), 0).astype(F32) + F32(at)
        for cc, ss, lo_lane, width in ((code_a, str_a, 0, extent), (code_b, str_b, extent, rows)):
            cb = [jnp.broadcast_to(cc[m : m + 1, :], (step, extent)) - sub for m in range(slots)]
            for k in range(classes):
                acc = jnp.zeros((step, extent), F32)
                for m in range(slots):
                    sm = jnp.broadcast_to(ss[m : m + 1, :], (step, extent))
                    acc = acc + jnp.where(cb[m] == F32(k * STRIDE), sm, F32(0.0))
                dpick[k * rows + at : k * rows + at + step, lo_lane : lo_lane + width] = acc[:, :width].astype(BF16)

    sums = [jnp.zeros((8, 128), F32) for _ in range(4)]
    near_band = pl.multiple_of((band + rows) * odd_cell, band)
    far_band = pl.multiple_of(rows * (1 - odd_cell), band)
    far_rows = pl.multiple_of(band * odd_cell, band)
    to_partner(0).wait_recv()
    forward(0).start()
    for p in range(pairs):
        if p + 1 < pairs:
            to_partner(p + 1).wait_recv()
            forward(p + 1).start()
        forward(p).wait_recv()
        around = jnp.concatenate(
            [
                near[p, pl.ds(near_band, band), :],
                send[p, 0:band, :],
                send[p, band + rows :, :],
                far[p, pl.ds(far_band, band), :],
            ],
            axis=0,
        )
        gs[...] = jnp.dot(pick[...], around, preferred_element_type=F32).astype(BF16)
        spread = jnp.concatenate(
            [near[p, band : band + rows, :], send[p, band : band + rows, :], far[p, pl.ds(far_rows, rows), :]], axis=0
        )
        whole = jnp.dot(dpick[...], spread, preferred_element_type=F32)
        hi = whole.astype(BF16)
        ghi[...] = hi
        glo[...] = (whole - hi.astype(F32)).astype(BF16)
        even = jnp.zeros((rows, STRIDE), F32)
        odd = jnp.zeros((rows, STRIDE), F32)
        deven = jnp.zeros((2 * rows, STRIDE), F32)
        dodd = jnp.zeros((2 * rows, STRIDE), F32)
        skip = wide - STRIDE
        for k in range(classes):
            r = slice(k * rows, (k + 1) * rows)
            even = even + jnp.dot(gs[r, 0:STRIDE], te[k], preferred_element_type=F32)
            odd = odd + jnp.dot(gs[r, skip:], to[k], preferred_element_type=F32)
            both = jnp.concatenate([ghi[r, :], glo[r, :]], axis=0)
            deven = deven + jnp.dot(both[:, 0:STRIDE], tet[k], preferred_element_type=F32)
            dodd = dodd + jnp.dot(both[:, skip:], tot[k], preferred_element_type=F32)
        de = deven[:rows] + deven[rows:]
        do = dodd[:rows] + dodd[rows:]
        mid = STRIDE - skip
        coupled = jnp.concatenate([even[:, :skip], even[:, skip:] + odd[:, :mid], odd[:, mid:]], axis=1)
        back = jnp.concatenate([de[:, :skip], de[:, skip:] + do[:, :mid], do[:, mid:]], axis=1)
        x = inc_ref[:, p * wide : (p + 1) * wide]
        image = x - gain[...] * coupled
        dual = x - back
        img_ref[:, p * wide : (p + 1) * wide] = image
        dual_ref[:, p * wide : (p + 1) * wide] = dual
        for copy in results_out(p):
            copy.start()
        sums[0] = sums[0] + folded(x * x)
        sums[1] = sums[1] + folded(x * image)
        sums[2] = sums[2] + folded(x * dual)
        sums[3] = sums[3] + folded(image * dual)

    mine = jnp.concatenate(
        [jnp.sum(s, axis=0, keepdims=True) for s in sums] + [jnp.zeros((4, 128), F32)], axis=0
    )
    red[here] = mine

    def sums_copy(t, slot):
        return pltpu.make_async_remote_copy(
            src_ref=red.at[slot],
            dst_ref=red.at[slot],
            send_sem=tssem.at[t],
            recv_sem=trsem.at[slot],
            device_id=peer(t)[0],
            device_id_type=pl.DeviceIdType.MESH,
        )

    def sums_start(t, c):
        sums_copy(t, here).start()
        return c

    def sums_wait(t, c):
        sums_copy(t, peer(t)[1]).wait_recv()
        return c

    lax.fori_loop(1, devices, sums_start, 0)
    lax.fori_loop(1, devices, sums_wait, 0)
    total = jnp.sum(jnp.sum(red[...], axis=0), axis=1, keepdims=True)
    norm_old = total[0:1]
    along_image = total[1:2]
    along_dual = total[2:3]
    cross = total[3:4]
    size = norm_old / along_image
    norm_new = norm_old - size * (along_image + along_dual) + size * size * cross
    ratio = norm_new / norm_old
    coef_ref[0:1, :] = jnp.broadcast_to(size, (1, 128))
    coef_ref[1:2, :] = jnp.broadcast_to(ratio, (1, 128))
    coef_ref[2:8, :] = jnp.zeros((6, 128), F32)

    meta_a.wait_send()
    meta_b.wait_send()
    for p in range(pairs):
        to_partner(p).wait_send()
        forward(p).wait_send()
        for copy in results_out(p):
            copy.wait()

    def sums_sent(t, c):
        sums_copy(t, here).wait_send()
        return c

    lax.fori_loop(1, devices, sums_sent, 0)


def finish(inc_ref, img_ref, dual_ref, coef_ref, sol_hbm, res_hbm, dres_hbm, dir_hbm, held, sem):
    rows, columns = inc_ref.shape
    size = coef_ref[0:1, 0:1]
    ratio = coef_ref[1:2, 0:1]
    copies = []
    step = rows // 4
    for b in range(4):
        cut = (slice(b * step, (b + 1) * step), slice(None))
        x = inc_ref[cut]
        residual = x - size * img_ref[cut]
        values = (size * x, residual, x - size * dual_ref[cut], residual + ratio * x)
        for i, (value, out) in enumerate(zip(values, (sol_hbm, res_hbm, dres_hbm, dir_hbm))):
            held[(i,) + cut] = value
            copy = pltpu.make_async_copy(held.at[(i,) + cut], out.at[cut], sem.at[i, b])
            copy.start()
            copies.append(copy)
    for copy in copies:
        copy.wait()


def on_device(cells, dirs, incident, scattering, translations, pair_sphere, pair_class, pair_weight, pair_mask):
    rows, columns = incident.shape
    classes, order, _ = translations.shape
    slots = pair_sphere.shape[1]
    anywhere = pl.BlockSpec(memory_space=pltpu.HBM)
    field = jax.ShapeDtypeStruct((rows, columns), F32)
    wide = 2 * order
    pairs = columns // wide
    vmem = pl.BlockSpec(memory_space=pltpu.VMEM)
    held = pl.pallas_call(
        functools.partial(kernel, cells, dirs),
        out_shape=(field,) * 2 + (jax.ShapeDtypeStruct((8, 128), F32),),
        in_specs=[anywhere] * 7,
        out_specs=(anywhere, anywhere, vmem),
        scratch_shapes=[
            pltpu.VMEM((rows, columns), F32),
            pltpu.VMEM((rows, columns), F32),
            pltpu.VMEM((rows, columns), F32),
            pltpu.VMEM((rows, order), F32),
            pltpu.VMEM((classes, order, order), BF16),
            pltpu.VMEM((slots, rows), jnp.int32),
            pltpu.VMEM((slots, rows), jnp.int32),
            pltpu.VMEM((slots, rows), BF16),
            pltpu.VMEM((slots, rows), jnp.int32),
            pltpu.VMEM((pairs, 2 * rows, wide), BF16),
            pltpu.VMEM((pairs, 2 * rows, wide), BF16),
            pltpu.VMEM((pairs, 3 * rows // 2, wide), BF16),
            pltpu.VMEM((2 * slots, 2 * rows), F32),
            pltpu.VMEM((2 * slots, 2 * rows), F32),
            pltpu.VMEM((2 * slots, 2 * rows), F32),
            pltpu.VMEM((rows, wide), F32),
            pltpu.VMEM((classes * rows, 2 * rows), BF16),
            pltpu.VMEM((classes * rows, 3 * rows), BF16),
            pltpu.VMEM((classes, STRIDE, STRIDE), BF16),
            pltpu.VMEM((classes, STRIDE, STRIDE), BF16),
            pltpu.VMEM((classes, STRIDE, STRIDE), BF16),
            pltpu.VMEM((classes, STRIDE, STRIDE), BF16),
            pltpu.VMEM((classes * rows, wide), BF16),
            pltpu.VMEM((classes * rows, wide), BF16),
            pltpu.VMEM((classes * rows, wide), BF16),
            pltpu.VMEM((cells * dirs, 8, 128), F32),
            pltpu.SemaphoreType.DMA((pairs,)),
            pltpu.SemaphoreType.DMA((2, pairs)),
            pltpu.SemaphoreType.DMA((6,)),
            pltpu.SemaphoreType.DMA((pairs,)),
            pltpu.SemaphoreType.DMA((pairs,)),
            pltpu.SemaphoreType.DMA((2,)),
            pltpu.SemaphoreType.DMA((2,)),
            pltpu.SemaphoreType.DMA((pairs,)),
            pltpu.SemaphoreType.DMA((pairs,)),
            pltpu.SemaphoreType.DMA((cells * dirs,)),
            pltpu.SemaphoreType.DMA((cells * dirs,)),
        ],
        compiler_params=pltpu.CompilerParams(
            collective_id=0, has_side_effects=True, vmem_limit_bytes=56 * 1024 * 1024
        ),
    )(incident, scattering, translations, pair_sphere.T, pair_class.T, pair_weight.T, pair_mask.T)
    return pl.pallas_call(
        finish,
        out_shape=(field,) * 4,
        in_specs=[vmem] * 4,
        out_specs=(anywhere,) * 4,
        scratch_shapes=[pltpu.VMEM((4, rows, columns), F32), pltpu.SemaphoreType.DMA((4, 4))],
    )(incident, *held)


def solution(mesh):
    cells, dirs = mesh.shape["cells"], mesh.shape["dirs"]
    split = P("cells", "dirs")
    by_cell = P("cells", None)
    return jax.shard_map(
        functools.partial(on_device, cells, dirs),
        mesh=mesh,
        in_specs=(split, by_cell, P(), by_cell, by_cell, by_cell, by_cell),
        out_specs=(split, split, split, split),
        check_vma=False,
    )
```

```python
import functools
import jax
import jax.numpy as jnp
from jax import lax
from jax.experimental import pallas as pl
from jax.experimental.pallas import tpu as pltpu
from jax.sharding import PartitionSpec as P

F32 = jnp.float32
BF16 = jnp.bfloat16
STRIDE = 256


def folded(x):
    rows, width = x.shape
    y = jnp.sum(x.reshape(rows // 8, 8, width), axis=0)
    out = y[:, :128]
    for at in range(128, width, 128):
        out = out + y[:, at : at + 128]
    return out


def kernel(
    cells,
    dirs,
    inc_hbm,
    sc_hbm,
    tr_hbm,
    ps_hbm,
    pc_hbm,
    pw_hbm,
    pm_hbm,
    img_hbm,
    dual_hbm,
    coef_ref,
    inc_ref,
    img_ref,
    dual_ref,
    sc_ref,
    tr_ref,
    ps_ref,
    pc_ref,
    pw_ref,
    pm_ref,
    send,
    near,
    far,
    meta,
    meta_near,
    meta_far,
    gain,
    pick,
    dpick,
    te,
    to,
    tet,
    tot,
    gs,
    ghi,
    glo,
    red,
    isem,
    osem,
    lsem,
    ssem,
    rsem,
    msem,
    mrsem,
    fssem,
    frsem,
    tssem,
    trsem,
):
    rows, columns = inc_ref.shape
    band = rows // 2
    classes, order, _ = tr_ref.shape
    slots = ps_ref.shape[0]
    wide = 2 * order
    pairs = columns // wide
    me = lax.axis_index("cells")
    my_dir = lax.axis_index("dirs")
    devices = cells * dirs
    here = me * dirs + my_dir
    odd_cell = lax.rem(me, 2)
    partner = me + 1 - 2 * odd_cell
    across = lax.rem(me - 1 + 2 * odd_cell + cells, cells)
    onward = lax.rem(me + 2 - 4 * odd_cell + cells, cells)

    def peer(t, d):
        cell = me + t
        side = my_dir + d
        return (jnp.where(cell >= cells, cell - cells, cell), jnp.where(side >= dirs, side - dirs, side))

    small = [
        pltpu.make_async_copy(a, b, lsem.at[i])
        for i, (a, b) in enumerate(
            (
                (sc_hbm, sc_ref),
                (ps_hbm, ps_ref),
                (pc_hbm, pc_ref),
                (pw_hbm, pw_ref),
                (pm_hbm, pm_ref),
                (tr_hbm, tr_ref),
            )
        )
    ]

    def incident_in(p):
        cut = (slice(None), slice(p * wide, (p + 1) * wide))
        return pltpu.make_async_copy(inc_hbm.at[cut], inc_ref.at[cut], isem.at[p])

    def results_out(p):
        cut = (slice(None), slice(p * wide, (p + 1) * wide))
        return (
            pltpu.make_async_copy(img_ref.at[cut], img_hbm.at[cut], osem.at[0, p]),
            pltpu.make_async_copy(dual_ref.at[cut], dual_hbm.at[cut], osem.at[1, p]),
        )

    barrier = pltpu.get_barrier_semaphore()

    for copy in small[:5]:
        copy.start()
    for p in range(pairs):
        incident_in(p).start()
    small[5].start()

    def greet(t, c):
        for d in range(dirs):
            pl.semaphore_signal(barrier, inc=1, device_id=peer(t, d), device_id_type=pl.DeviceIdType.MESH)
        return c

    for d in range(1, dirs):
        pl.semaphore_signal(barrier, inc=1, device_id=peer(0, d), device_id_type=pl.DeviceIdType.MESH)
    lax.fori_loop(1, cells, greet, 0)

    for copy in small[1:5]:
        copy.wait()
    ps = ps_ref[...]
    owner = ps // rows
    within = ps - owner * rows
    is_own = owner == me
    is_near = owner == partner
    code = (
        pc_ref[...] * STRIDE + jnp.where(is_near, within, jnp.where(is_own, rows + within, 2 * rows + within))
    ).astype(F32)
    place = jnp.where(
        is_near,
        within - band * odd_cell,
        jnp.where(is_own, band + within, rows + band + within - band * (1 - odd_cell)),
    )
    column = (pc_ref[...] * STRIDE + place).astype(F32)
    strength = pw_ref[...].astype(F32) * pm_ref[...].astype(F32)
    meta[0:slots, :] = jnp.concatenate([code, code], axis=1)
    meta[slots : 2 * slots, :] = jnp.concatenate([strength, strength], axis=1)

    small[0].wait()
    gain[:, 0:order] = sc_ref[...]
    gain[:, order:wide] = sc_ref[...]
    g = gain[...]

    def fill(p):
        incident_in(p).wait()
        x = inc_ref[:, p * wide : (p + 1) * wide]
        src = x.astype(BF16)
        send[p, 0:band, :] = src[0:band]
        send[p, band : band + rows, :] = (g * x).astype(BF16)
        send[p, band + rows :, :] = src[band:]

    fill(0)
    pl.semaphore_wait(barrier, devices - 1)

    def to_partner(p):
        return pltpu.make_async_remote_copy(
            src_ref=send.at[p],
            dst_ref=near.at[p],
            send_sem=ssem.at[p],
            recv_sem=rsem.at[p],
            device_id=(partner, my_dir),
            device_id_type=pl.DeviceIdType.MESH,
        )

    pass_on = pl.multiple_of(band * (1 - odd_cell), band)

    def forward(p):
        return pltpu.make_async_remote_copy(
            src_ref=near.at[p, pl.ds(pass_on, band + rows), :],
            dst_ref=far.at[p],
            send_sem=fssem.at[p],
            recv_sem=frsem.at[p],
            device_id=(onward, my_dir),
            device_id_type=pl.DeviceIdType.MESH,
        )

    def meta_copy(i, dst, who):
        return pltpu.make_async_remote_copy(
            src_ref=meta,
            dst_ref=dst,
            send_sem=msem.at[i],
            recv_sem=mrsem.at[i],
            device_id=(who, my_dir),
            device_id_type=pl.DeviceIdType.MESH,
        )

    meta_a = meta_copy(0, meta_near, partner)
    meta_b = meta_copy(1, meta_far, across)
    meta_b.start()
    meta_a.start()
    for p in range(pairs):
        if p > 0:
            fill(p)
        to_partner(p).start()

    both = jnp.concatenate([column, strength], axis=0)
    both = jnp.concatenate([both, both], axis=1)
    flat = jnp.concatenate([both] * (128 // (2 * slots)), axis=0).T
    code = flat[0:rows, 0:slots]
    strength = flat[0:rows, slots : 2 * slots]
    small[5].wait()

    gap = STRIDE - order

    def place_class(k, c):
        te[k] = jnp.zeros((STRIDE, STRIDE), BF16)
        te[k, 0:order, 0:order] = tr_ref[k]
        full = te[k].astype(F32)
        to[k] = pltpu.roll(pltpu.roll(full, gap, 0), gap, 1).astype(BF16)
        turned = full.T
        tet[k] = turned.astype(BF16)
        tot[k] = pltpu.roll(pltpu.roll(turned, gap, 0), gap, 1).astype(BF16)
        return c

    lax.fori_loop(0, classes, place_class, 0)

    def receive(p):
        to_partner(p).wait_recv()
        forward(p).start()

    receive(0)
    extent = rows + 2 * band
    step = 16
    lane = lax.broadcasted_iota(jnp.int32, (step, extent), 1).astype(F32)
    for b in range(rows // step):
        at = b * step
        cb = [jnp.broadcast_to(code[at : at + step, m : m + 1], (step, extent)) - lane for m in range(slots)]
        sb = [jnp.broadcast_to(strength[at : at + step, m : m + 1], (step, extent)) for m in range(slots)]
        for k in range(classes):
            acc = jnp.zeros((step, extent), F32)
            for m in range(slots):
                acc = acc + jnp.where(cb[m] == F32(k * STRIDE), sb[m], F32(0.0))
            pick[k * rows + at : k * rows + at + step, :] = acc.astype(BF16)

    receive(1)
    meta_a.wait_recv()
    meta_b.wait_recv()
    low = lax.broadcasted_iota(jnp.int32, (slots, extent), 1) < rows
    code_a = jnp.where(low, meta_near[0:slots, :], meta[0:slots, :] - F32(rows))
    str_a = jnp.where(low, meta_near[slots : 2 * slots, :], meta[slots : 2 * slots, :])
    code_b = meta_far[0:slots, :] - F32(2 * rows)
    str_b = meta_far[slots : 2 * slots, :]
    for b in range(rows // step):
        at = b * step
        sub = lax.broadcasted_iota(jnp.int32, (step, extent), 0).astype(F32) + F32(at)
        for cc, ss, lo_lane, width in ((code_a, str_a, 0, extent), (code_b, str_b, extent, rows)):
            cb = [jnp.broadcast_to(cc[m : m + 1, :], (step, extent)) - sub for m in range(slots)]
            for k in range(classes):
                acc = jnp.zeros((step, extent), F32)
                for m in range(slots):
                    sm = jnp.broadcast_to(ss[m : m + 1, :], (step, extent))
                    acc = acc + jnp.where(cb[m] == F32(k * STRIDE), sm, F32(0.0))
                dpick[k * rows + at : k * rows + at + step, lo_lane : lo_lane + width] = acc[:, :width].astype(BF16)

    sums = [jnp.zeros((8, 128), F32) for _ in range(4)]
    near_band = pl.multiple_of((band + rows) * odd_cell, band)
    far_band = pl.multiple_of(rows * (1 - odd_cell), band)
    far_rows = pl.multiple_of(band * odd_cell, band)
    receive(2)
    for p in range(pairs):
        if p + 3 < pairs:
            receive(p + 3)
        forward(p).wait_recv()
        around = jnp.concatenate(
            [
                near[p, pl.ds(near_band, band), :],
                send[p, 0:band, :],
                send[p, band + rows :, :],
                far[p, pl.ds(far_band, band), :],
            ],
            axis=0,
        )
        gs[...] = jnp.dot(pick[...], around, preferred_element_type=F32).astype(BF16)
        spread = jnp.concatenate(
            [near[p, band : band + rows, :], send[p, band : band + rows, :], far[p, pl.ds(far_rows, rows), :]], axis=0
        )
        whole = jnp.dot(dpick[...], spread, preferred_element_type=F32)
        hi = whole.astype(BF16)
        ghi[...] = hi
        glo[...] = (whole - hi.astype(F32)).astype(BF16)
        even = jnp.zeros((rows, STRIDE), F32)
        odd = jnp.zeros((rows, STRIDE), F32)
        deven = jnp.zeros((2 * rows, STRIDE), F32)
        dodd = jnp.zeros((2 * rows, STRIDE), F32)
        skip = wide - STRIDE
        for k in range(classes):
            r = slice(k * rows, (k + 1) * rows)
            even = even + jnp.dot(gs[r, 0:STRIDE], te[k], preferred_element_type=F32)
            odd = odd + jnp.dot(gs[r, skip:], to[k], preferred_element_type=F32)
            both = jnp.concatenate([ghi[r, :], glo[r, :]], axis=0)
            deven = deven + jnp.dot(both[:, 0:STRIDE], tet[k], preferred_element_type=F32)
            dodd = dodd + jnp.dot(both[:, skip:], tot[k], preferred_element_type=F32)
        de = deven[:rows] + deven[rows:]
        do = dodd[:rows] + dodd[rows:]
        mid = STRIDE - skip
        coupled = jnp.concatenate([even[:, :skip], even[:, skip:] + odd[:, :mid], odd[:, mid:]], axis=1)
        back = jnp.concatenate([de[:, :skip], de[:, skip:] + do[:, :mid], do[:, mid:]], axis=1)
        x = inc_ref[:, p * wide : (p + 1) * wide]
        image = x - gain[...] * coupled
        dual = x - back
        img_ref[:, p * wide : (p + 1) * wide] = image
        dual_ref[:, p * wide : (p + 1) * wide] = dual
        for copy in results_out(p):
            copy.start()
        sums[0] = sums[0] + folded(x * x)
        sums[1] = sums[1] + folded(x * image)
        sums[2] = sums[2] + folded(x * dual)
        sums[3] = sums[3] + folded(image * dual)

    mine = jnp.concatenate(
        [jnp.sum(s, axis=0, keepdims=True) for s in sums] + [jnp.zeros((4, 128), F32)], axis=0
    )
    red[here] = mine

    def sums_copy(t, d):
        return pltpu.make_async_remote_copy(
            src_ref=red.at[here],
            dst_ref=red.at[here],
            send_sem=tssem,
            recv_sem=trsem,
            device_id=peer(t, d),
            device_id_type=pl.DeviceIdType.MESH,
        )

    def sums_start(t, c):
        for d in range(dirs):
            sums_copy(t, d).start()
        return c

    others = red.at[0 : devices - 1]
    lax.fori_loop(1, cells, sums_start, 0)
    for d in range(1, dirs):
        sums_copy(0, d).start()
    pltpu.make_async_copy(others, others, trsem).wait()
    total = jnp.sum(jnp.sum(red[...], axis=0), axis=1, keepdims=True)
    norm_old = total[0:1]
    along_image = total[1:2]
    along_dual = total[2:3]
    cross = total[3:4]
    size = norm_old / along_image
    norm_new = norm_old - size * (along_image + along_dual) + size * size * cross
    ratio = norm_new / norm_old
    coef_ref[0:1, :] = jnp.broadcast_to(size, (1, 128))
    coef_ref[1:2, :] = jnp.broadcast_to(ratio, (1, 128))
    coef_ref[2:8, :] = jnp.zeros((6, 128), F32)

    meta_a.wait_send()
    meta_b.wait_send()
    for p in range(pairs):
        to_partner(p).wait_send()
        forward(p).wait_send()
        for copy in results_out(p):
            copy.wait()

    pltpu.make_async_copy(others, others, tssem).wait()


def finish(inc_ref, img_ref, dual_ref, coef_ref, sol_hbm, res_hbm, dres_hbm, dir_hbm, held, sem):
    rows, columns = inc_ref.shape
    size = coef_ref[0:1, 0:1]
    ratio = coef_ref[1:2, 0:1]
    copies = []
    step = rows // 4
    for b in range(4):
        cut = (slice(b * step, (b + 1) * step), slice(None))
        x = inc_ref[cut]
        residual = x - size * img_ref[cut]
        values = (size * x, residual, x - size * dual_ref[cut], residual + ratio * x)
        for i, (value, out) in enumerate(zip(values, (sol_hbm, res_hbm, dres_hbm, dir_hbm))):
            held[(i,) + cut] = value
            copy = pltpu.make_async_copy(held.at[(i,) + cut], out.at[cut], sem.at[i, b])
            copy.start()
            copies.append(copy)
    for copy in copies:
        copy.wait()


def on_device(cells, dirs, incident, scattering, translations, pair_sphere, pair_class, pair_weight, pair_mask):
    rows, columns = incident.shape
    classes, order, _ = translations.shape
    slots = pair_sphere.shape[1]
    anywhere = pl.BlockSpec(memory_space=pltpu.HBM)
    field = jax.ShapeDtypeStruct((rows, columns), F32)
    wide = 2 * order
    pairs = columns // wide
    vmem = pl.BlockSpec(memory_space=pltpu.VMEM)
    held = pl.pallas_call(
        functools.partial(kernel, cells, dirs),
        out_shape=(field,) * 2 + (jax.ShapeDtypeStruct((8, 128), F32),),
        in_specs=[anywhere] * 7,
        out_specs=(anywhere, anywhere, vmem),
        scratch_shapes=[
            pltpu.VMEM((rows, columns), F32),
            pltpu.VMEM((rows, columns), F32),
            pltpu.VMEM((rows, columns), F32),
            pltpu.VMEM((rows, order), F32),
            pltpu.VMEM((classes, order, order), BF16),
            pltpu.VMEM((slots, rows), jnp.int32),
            pltpu.VMEM((slots, rows), jnp.int32),
            pltpu.VMEM((slots, rows), BF16),
            pltpu.VMEM((slots, rows), jnp.int32),
            pltpu.VMEM((pairs, 2 * rows, wide), BF16),
            pltpu.VMEM((pairs, 2 * rows, wide), BF16),
            pltpu.VMEM((pairs, 3 * rows // 2, wide), BF16),
            pltpu.VMEM((2 * slots, 2 * rows), F32),
            pltpu.VMEM((2 * slots, 2 * rows), F32),
            pltpu.VMEM((2 * slots, 2 * rows), F32),
            pltpu.VMEM((rows, wide), F32),
            pltpu.VMEM((classes * rows, 2 * rows), BF16),
            pltpu.VMEM((classes * rows, 3 * rows), BF16),
            pltpu.VMEM((classes, STRIDE, STRIDE), BF16),
            pltpu.VMEM((classes, STRIDE, STRIDE), BF16),
            pltpu.VMEM((classes, STRIDE, STRIDE), BF16),
            pltpu.VMEM((classes, STRIDE, STRIDE), BF16),
            pltpu.VMEM((classes * rows, wide), BF16),
            pltpu.VMEM((classes * rows, wide), BF16),
            pltpu.VMEM((classes * rows, wide), BF16),
            pltpu.VMEM((cells * dirs, 8, 128), F32),
            pltpu.SemaphoreType.DMA((pairs,)),
            pltpu.SemaphoreType.DMA((2, pairs)),
            pltpu.SemaphoreType.DMA((6,)),
            pltpu.SemaphoreType.DMA((pairs,)),
            pltpu.SemaphoreType.DMA((pairs,)),
            pltpu.SemaphoreType.DMA((2,)),
            pltpu.SemaphoreType.DMA((2,)),
            pltpu.SemaphoreType.DMA((pairs,)),
            pltpu.SemaphoreType.DMA((pairs,)),
            pltpu.SemaphoreType.DMA,
            pltpu.SemaphoreType.DMA,
        ],
        compiler_params=pltpu.CompilerParams(
            collective_id=0, has_side_effects=True, vmem_limit_bytes=56 * 1024 * 1024
        ),
    )(incident, scattering, translations, pair_sphere.T, pair_class.T, pair_weight.T, pair_mask.T)
    return pl.pallas_call(
        finish,
        out_shape=(field,) * 4,
        in_specs=[vmem] * 4,
        out_specs=(anywhere,) * 4,
        scratch_shapes=[pltpu.VMEM((4, rows, columns), F32), pltpu.SemaphoreType.DMA((4, 4))],
    )(incident, *held)


def solution(mesh):
    cells, dirs = mesh.shape["cells"], mesh.shape["dirs"]
    split = P("cells", "dirs")
    by_cell = P("cells", None)
    return jax.shard_map(
        functools.partial(on_device, cells, dirs),
        mesh=mesh,
        in_specs=(split, by_cell, P(), by_cell, by_cell, by_cell, by_cell),
        out_specs=(split, split, split, split),
        check_vma=False,
    )
```
